512 devices in a mesh: gx: 32 (over z, core), yz: 16 (over y, x).
Axes of the slice: x: 4, y: 4, z: 16, core: 2. Of those that a mesh axis runs over, the one named last changes fastest.
Arguments:
- slab: float32 [500, 480, 2048], P(None, 'gx', 'yz'), may hold values from -80 to 80, as said below
- factor_one: float32 [500, 96], replicated, may hold values from -0.25 to 0.25
Outputs:
- contracted: float32 [96, 480, 2048], P('gx', None, 'yz')
- lower_factor: float32 [480, 480], replicated
The draws below stay inside these ranges and needn't reach their ends.
Inputs may be any that keep to these rules, and one draw needn't show every extreme that they name: `slab`: real-valued entries.
All inputs are finite; a program needn't handle non-finite values.
Results may differ from the reference program's by a relative error of at most 0.000082.
Values sent between devices are 32-bit elements; how exact they have to be, the bound alone decides.
A program may use at most 128 MiB of HBM per device.

```python
import jax
import jax.numpy as jnp
from jax import lax

I1 = 500
I2 = 480
R1 = 96
CELLS = 2048


def draw_slab(key, part):
    key = jax.random.fold_in(key, 11)
    key_main, key_latent, key_load, key_scale = jax.random.split(key, 4)
    latent_count = 48
    main_part = jax.random.truncated_normal(key_main, -4.0, 4.0, (I1, I2, CELLS), jnp.float32)
    latent = jax.random.truncated_normal(key_latent, -4.0, 4.0, (I1, latent_count, CELLS), jnp.float32)
    loadings = jax.random.truncated_normal(key_load, -4.0, 4.0, (I2, latent_count), jnp.float32)
    weight_common = 0.7
    common = jnp.einsum('ikc,jk->ijc', latent, loadings, precision=lax.Precision.HIGHEST)
    common = common * jnp.float32(weight_common / latent_count ** 0.5)
    common = 4.0 * jnp.tanh(common / 4.0)
    scales = jnp.exp(jax.random.uniform(key_scale, (1, I2, 1), jnp.float32, 0.0, 2.302585))
    return (scales * (main_part + common)).astype(jnp.float32)


def bell_draw(stream_key, shape, width, most, dtype=jnp.bfloat16):
    return jnp.clip(width * jax.random.normal(stream_key, shape, jnp.float32), -most, most).astype(dtype)


def setup_inputs(seed: int = 0) -> dict:
    splits = jax.random.split(jax.random.key(seed), 3)
    return {
        "slab": draw_slab(jax.random.fold_in(splits[2], 71), 0),
        "factor_one": bell_draw(splits[1], (I1, R1), I1 ** -0.5, 0.25, jnp.float32),
    }


def reference(slab, factor_one):
    contracted = jnp.einsum('ir,ijc->rjc', factor_one, slab, precision=lax.Precision.HIGHEST)
    gram = jnp.einsum('rjc,rkc->jk', contracted, contracted, precision=lax.Precision.HIGHEST)
    gram = gram / jnp.float32(R1 * CELLS)
    lower_factor = jnp.linalg.cholesky(gram)
    return (contracted, lower_factor)
```

```python
import jax
import jax.numpy as jnp
from jax import lax
from jax.experimental import pallas as pl
from jax.experimental.pallas import tpu as pltpu
from jax.sharding import PartitionSpec as P

I1, I2, R1 = 500, 480, 96
GX, YZ = 32, 16
KPAD = 512
JB = I2 // GX
RB = R1 // GX
LANES = 128
COLS = (0, 480, 832, 1056)
PACKED = 1152
PIECE = PACKED // YZ
TILES = PIECE // 8
BF = jnp.bfloat16
F32 = jnp.float32


def split(x):
    hi = x.astype(BF)
    return hi, (x - hi.astype(F32)).astype(BF)


def dot(a, b):
    return lax.dot_general(a, b, (((1,), (0,)), ((), ())), preferred_element_type=F32)


def dot_nt(a, b):
    return lax.dot_general(a, b, (((1,), (1,)), ((), ())), preferred_element_type=F32)


def far_first(me, k, n):
    step = (k + 1) // 2
    off = n // 2 + jnp.where(k % 2 == 1, -step, step)
    return lax.rem(me + off, n)


def exchange_kernel(
    slab, ft, con, full,
    slab_a, slab_b, ft_in, ft_v, send_a, send_b, got_a, got_b, gram, got_y, mine, got_z, total,
    load_sem, sa_sem, ra_sem, sb_sem, rb_sem, sy_sem, ry_sem, sz_sem, rz_sem, sg_sem, rg_sem, sf_sem, rf_sem,
):
    gx = lax.axis_index("gx")
    yz = lax.axis_index("yz")

    load_f = pltpu.make_async_copy(ft, ft_in, load_sem.at[2])
    load_a = pltpu.make_async_copy(slab.at[pl.ds(0, 8)], slab_a.at[:, pl.ds(0, I1), :], load_sem.at[0])
    load_b = pltpu.make_async_copy(slab.at[pl.ds(8, JB - 8)], slab_b.at[:, pl.ds(0, I1), :], load_sem.at[1])
    load_f.start()
    load_a.start()
    load_b.start()

    barrier = pltpu.get_barrier_semaphore()

    @pl.loop(1, GX)
    def _(d):
        pl.semaphore_signal(barrier, inc=1, device_id={"gx": lax.rem(gx + d, GX)}, device_id_type=pl.DeviceIdType.MESH)

    @pl.loop(1, YZ)
    def _(d):
        pl.semaphore_signal(barrier, inc=1, device_id={"yz": lax.rem(yz + d, YZ)}, device_id_type=pl.DeviceIdType.MESH)

    slab_a[:, pl.ds(I1, KPAD - I1), :] = jnp.zeros((8, KPAD - I1, LANES), F32)
    slab_b[:, pl.ds(I1, KPAD - I1), :] = jnp.zeros((JB - 8, KPAD - I1, LANES), F32)
    ft_v[:, pl.ds(KPAD - LANES, LANES)] = jnp.zeros((R1, LANES), F32)
    gram[pl.ds(COLS[3], PACKED - COLS[3]), :] = jnp.zeros((PACKED - COLS[3], LANES), F32)
    load_f.wait()
    ft_v[:, pl.ds(0, I1)] = ft_in[...]
    f_hi, f_lo = split(ft_v[...])
    f_both = jnp.concatenate([f_hi, f_lo], axis=0)

    def contract(src, dst, count):
        for j in range(0, count, 2):
            js = [j] if j + 1 == count else [j, j + 1]
            s = [src[q] for q in js]
            s = s[0] if len(s) == 1 else jnp.concatenate(s, axis=1)
            s_hi, s_lo = split(s)
            two = dot(f_both, s_hi)
            res = two[:R1] + (two[R1:] + dot(f_hi, s_lo))
            for n, q in enumerate(js):
                dst[:, q, :] = res[:, n * LANES:(n + 1) * LANES]

    def copy_a(to):
        return pltpu.make_async_remote_copy(
            src_ref=send_a.at[pl.ds(to * RB, RB)], dst_ref=got_a.at[gx],
            send_sem=sa_sem.at[to], recv_sem=ra_sem.at[gx],
            device_id={"gx": to}, device_id_type=pl.DeviceIdType.MESH)

    def copy_b(to):
        return pltpu.make_async_remote_copy(
            src_ref=send_b.at[pl.ds(to * RB, RB)], dst_ref=got_b.at[gx],
            send_sem=sb_sem.at[to], recv_sem=rb_sem.at[gx],
            device_id={"gx": to}, device_id_type=pl.DeviceIdType.MESH)

    def from_a(at):
        return pltpu.make_async_remote_copy(
            src_ref=send_a.at[pl.ds(at * RB, RB)], dst_ref=got_a.at[at],
            send_sem=sa_sem.at[at], recv_sem=ra_sem.at[at],
            device_id={"gx": at}, device_id_type=pl.DeviceIdType.MESH)

    def from_b(at):
        return pltpu.make_async_remote_copy(
            src_ref=send_b.at[pl.ds(at * RB, RB)], dst_ref=got_b.at[at],
            send_sem=sb_sem.at[at], recv_sem=rb_sem.at[at],
            device_id={"gx": at}, device_id_type=pl.DeviceIdType.MESH)

    load_a.wait()
    contract(slab_a, send_a, 8)
    pl.semaphore_wait(barrier, GX - 1 + YZ - 1)

    @pl.loop(0, GX - 1)
    def _(k):
        copy_a(far_first(gx, k, GX)).start()

    load_b.wait()
    contract(slab_b, send_b, JB - 8)

    @pl.loop(0, GX - 1)
    def _(k):
        copy_b(far_first(gx, k, GX)).start()

    got_a[gx] = send_a[pl.ds(gx * RB, RB)]
    got_b[gx] = send_b[pl.ds(gx * RB, RB)]

    @pl.loop(1, GX)
    def _(d):
        at = lax.rem(gx + d, GX)
        from_a(at).wait_recv()
        from_b(at).wait_recv()

    for s in range(GX):
        for r in range(RB):
            con[r, pl.ds(JB * s, 8), :] = got_a[s, r]
            con[r, pl.ds(JB * s + 8, JB - 8), :] = got_b[s, r]

    hi, lo = split(jnp.concatenate([con[r] for r in range(RB)], axis=1))
    for c, at in enumerate(COLS):
        rows = I2 - LANES * c
        a = slice(LANES * c, I2)
        b = slice(LANES * c, min(LANES * (c + 1), I2))
        gram[pl.ds(at, rows), pl.ds(0, min(rows, LANES))] = dot_nt(hi[a], hi[b]) + (dot_nt(hi[a], lo[b]) + dot_nt(lo[a], hi[b]))

    def copy_y(to):
        return pltpu.make_async_remote_copy(
            src_ref=gram.at[pl.ds(pl.multiple_of(to * PIECE, 8), PIECE)], dst_ref=got_y.at[yz],
            send_sem=sy_sem.at[to], recv_sem=ry_sem.at[yz],
            device_id={"yz": to}, device_id_type=pl.DeviceIdType.MESH)

    def from_y(at):
        return pltpu.make_async_remote_copy(
            src_ref=gram.at[pl.ds(pl.multiple_of(at * PIECE, 8), PIECE)], dst_ref=got_y.at[at],
            send_sem=sy_sem.at[at], recv_sem=ry_sem.at[at],
            device_id={"yz": at}, device_id_type=pl.DeviceIdType.MESH)

    @pl.loop(1, YZ)
    def _(d):
        copy_y(lax.rem(yz + d, YZ)).start()

    got_y[yz] = gram[pl.ds(pl.multiple_of(yz * PIECE, 8), PIECE), :]

    @pl.loop(1, YZ)
    def _(d):
        from_y(lax.rem(yz + d, YZ)).wait_recv()

    mine[...] = jnp.sum(got_y[...], axis=0)

    def copy_z(t):
        return pltpu.make_async_remote_copy(
            src_ref=mine.at[pl.ds(pl.multiple_of(t * 8, 8), 8)], dst_ref=got_z.at[gx],
            send_sem=sz_sem.at[t], recv_sem=rz_sem.at[gx],
            device_id={"gx": 3 * t}, device_id_type=pl.DeviceIdType.MESH)

    def from_z(at):
        return pltpu.make_async_remote_copy(
            src_ref=mine.at[pl.ds(0, 8)], dst_ref=got_z.at[at],
            send_sem=sz_sem.at[0], recv_sem=rz_sem.at[at],
            device_id={"gx": at}, device_id_type=pl.DeviceIdType.MESH)

    owner = jnp.logical_and(lax.rem(gx, 3) == 0, gx < 3 * TILES)
    tile = gx // 3

    @pl.loop(0, TILES)
    def _(t):
        @pl.when(gx != 3 * t)
        def _():
            copy_z(t).start()

    def spread(to):
        return pltpu.make_async_remote_copy(
            src_ref=total.at[tile], dst_ref=total.at[tile],
            send_sem=sg_sem.at[to], recv_sem=rg_sem.at[tile],
            device_id={"gx": to}, device_id_type=pl.DeviceIdType.MESH)

    def from_owner(t):
        return pltpu.make_async_remote_copy(
            src_ref=total.at[t], dst_ref=total.at[t],
            send_sem=sg_sem.at[0], recv_sem=rg_sem.at[t],
            device_id={"gx": 3 * t}, device_id_type=pl.DeviceIdType.MESH)

    @pl.when(owner)
    def _():
        got_z[gx] = mine[pl.ds(pl.multiple_of(tile * 8, 8), 8), :]

        @pl.loop(1, GX)
        def _(d):
            from_z(lax.rem(gx + d, GX)).wait_recv()

        total[tile] = jnp.sum(got_z[...], axis=0) * (1.0 / (R1 * 2048))

        @pl.loop(0, GX - 1)
        def _(k):
            spread(far_first(gx, k, GX)).start()

    @pl.loop(0, TILES)
    def _(t):
        @pl.when(gx != 3 * t)
        def _():
            from_owner(t).wait_recv()

    def copy_f(to):
        return pltpu.make_async_remote_copy(
            src_ref=total, dst_ref=full.at[yz],
            send_sem=sf_sem.at[to], recv_sem=rf_sem.at[yz],
            device_id={"yz": to}, device_id_type=pl.DeviceIdType.MESH)

    def from_f(at):
        return pltpu.make_async_remote_copy(
            src_ref=total, dst_ref=full.at[at],
            send_sem=sf_sem.at[at], recv_sem=rf_sem.at[at],
            device_id={"yz": at}, device_id_type=pl.DeviceIdType.MESH)

    @pl.loop(1, YZ)
    def _(d):
        copy_f(lax.rem(yz + d, YZ)).start()

    full[yz] = total[...]

    @pl.loop(1, YZ)
    def _(d):
        from_f(lax.rem(yz + d, YZ)).wait_recv()

    @pl.loop(1, GX)
    def _(d):
        to = lax.rem(gx + d, GX)
        copy_a(to).wait_send()
        copy_b(to).wait_send()

        @pl.when(owner)
        def _():
            spread(to).wait_send()

    @pl.loop(1, YZ)
    def _(d):
        to = lax.rem(yz + d, YZ)
        copy_y(to).wait_send()
        copy_f(to).wait_send()

    @pl.loop(0, TILES)
    def _(t):
        @pl.when(gx != 3 * t)
        def _():
            copy_z(t).wait_send()


def exchange(slab, ft):
    dma = pltpu.SemaphoreType.DMA
    return pl.pallas_call(
        exchange_kernel,
        name="exchange",
        out_shape=(
            jax.ShapeDtypeStruct((RB, I2, LANES), F32),
            jax.ShapeDtypeStruct((YZ, TILES, 8, LANES), F32),
        ),
        in_specs=[pl.BlockSpec(memory_space=pltpu.HBM)] * 2,
        out_specs=(pl.BlockSpec(memory_space=pltpu.VMEM),) * 2,
        scratch_shapes=[
            pltpu.VMEM((8, KPAD, LANES), F32),
            pltpu.VMEM((JB - 8, KPAD, LANES), F32),
            pltpu.VMEM((R1, I1), F32),
            pltpu.VMEM((R1, KPAD), F32),
            pltpu.VMEM((R1, 8, LANES), F32),
            pltpu.VMEM((R1, JB - 8, LANES), F32),
            pltpu.VMEM((GX, RB, 8, LANES), F32),
            pltpu.VMEM((GX, RB, JB - 8, LANES), F32),
            pltpu.VMEM((PACKED, LANES), F32),
            pltpu.VMEM((YZ, PIECE, LANES), F32),
            pltpu.VMEM((PIECE, LANES), F32),
            pltpu.VMEM((GX, 8, LANES), F32),
            pltpu.VMEM((TILES, 8, LANES), F32),
            dma((3,)),
            dma((GX,)), dma((GX,)), dma((GX,)), dma((GX,)),
            dma((YZ,)), dma((YZ,)),
            dma((TILES,)), dma((GX,)),
            dma((GX,)), dma((TILES,)),
            dma((YZ,)), dma((YZ,)),
        ],
        compiler_params=pltpu.CompilerParams(
            collective_id=0, has_side_effects=True, vmem_limit_bytes=40 * 2**20
        ),
    )(slab, ft)


def outer(a, b):
    ah, al = split(a)
    bh, bl = split(b)
    lhs = jnp.concatenate([ah, ah, al], axis=0)
    rhs = jnp.concatenate([bh, bl, bh], axis=0)
    return lax.dot_general(lhs, rhs, (((0,), (0,)), ((), ())), preferred_element_type=F32)

def factor_rows(diag, rest, lane):
    tiles = [diag] + rest
    rows = [[x[8*p:8*p+8] for p in range(4)] for x in tiles]
    sub = lax.broadcasted_iota(jnp.int32, (8, LANES), 0)
    done = [[] for _ in tiles]
    for p in range(4):
        cols = [[jnp.broadcast_to(rows[0][q][:, lane+8*p+k:lane+8*p+k+1], (8, LANES)) for q in range(p, 4)] for k in range(8)]
        fin = [rows[t][p] for t in range(len(tiles))]
        for k in range(8):
            rs = lax.rsqrt(jnp.broadcast_to(cols[k][0][k:k+1], (8, LANES)))
            m = [c * rs for c in cols[k]]
            m0 = jnp.where(sub > k, m[0], 0.0)
            for kk in range(k+1, 8):
                w = jnp.broadcast_to(m[0][kk:kk+1], (8, LANES))
                cols[kk] = [cols[kk][0] - m0 * w] + [cols[kk][q] - m[q] * w for q in range(1, len(m))]
            for t in range(len(tiles)):
                r = jnp.broadcast_to(rows[t][p][k:k+1], (8, LANES)) * rs
                fin[t] = jnp.where(sub == k, r, fin[t])
                rows[t][p] = rows[t][p] - m0 * r
                for q in range(p+1, 4):
                    rows[t][q] = rows[t][q] - m[q-p] * r
        for t in range(len(tiles)):
            done[t].append(fin[t])
    return [jnp.concatenate(d, axis=0) for d in done]

def chol_kernel(packed, con, out, con_out, A, sem):
    copy = pltpu.make_async_copy(con, con_out, sem)
    copy.start()
    for c in range(4):
        n = I2 - 128*c
        for t in range(c, 4):
            rows = min(128, I2 - 128*t)
            blk = packed[pl.ds(COLS[c] + 128*(t-c), rows), :]
            if rows < 128:
                blk = jnp.concatenate([blk, jnp.zeros((128-rows, 128), F32)], axis=0)
            blk = blk.T
            if c == 3:
                i = lax.broadcasted_iota(jnp.int32, (128,128), 0)
                j = lax.broadcasted_iota(jnp.int32, (128,128), 1)
                ok = (i < 96) & (j < 96)
                blk = jnp.where(ok, blk, (i == j).astype(F32))
            A[t, pl.ds(128*c, 128), :] = blk
        for t in range(c):
            A[t, pl.ds(128*c, 128), :] = jnp.zeros((128,128), F32)

    @pl.loop(0, 4)
    def _(c):
        base = pl.multiple_of(c*128, 128)
        for sb in range(4):
            r0 = pl.multiple_of(base + 32*sb, 32)
            diag = A[c, pl.ds(r0, 32), :]
            rest = [A[t, pl.ds(r0, 32), :] for t in range(1, 4)]
            u = factor_rows(diag, rest, 32*sb)
            for t in range(1, 4):
                A[t, pl.ds(r0, 32), :] = u[t]
            A[c, pl.ds(r0, 32), :] = u[0]
            if sb < 3:
                upd = outer(u[0][:, 32*(sb+1):], jnp.concatenate(u[1:], axis=1))
                upd0 = outer(u[0][:, 32*(sb+1):], u[0])
                n = 128 - 32*(sb+1)
                new0 = A[c, pl.ds(r0+32, n), :] - upd0
                for t in range(1, 4):
                    A[t, pl.ds(r0+32, n), :] = A[t, pl.ds(r0+32, n), :] - upd[:, 128*(t-1):128*t]
                A[c, pl.ds(r0+32, n), :] = new0

        @pl.loop(c+1, 4)
        def _(d):
            lhs = A[d, pl.ds(base, 128), :]
            rhs = jnp.concatenate([A[t, pl.ds(base, 128), :] for t in range(1, 4)], axis=1)
            upd = outer(lhs, rhs)
            at = pl.multiple_of(d*128, 128)
            for t in range(1, 4):
                A[t, pl.ds(at, 128), :] = A[t, pl.ds(at, 128), :] - upd[:, 128*(t-1):128*t]

    for c in range(4):
        n = min(128, I2 - 128*c)
        for t in range(4):
            w = min(128, I2 - 128*t)
            if t > c:
                out[pl.ds(128*c, n), pl.ds(128*t, w)] = jnp.zeros((n, w), F32)
            else:
                blk = A[c, pl.ds(128*t, 128), :].T
                if t == c:
                    i = lax.broadcasted_iota(jnp.int32, (128,128), 0)
                    j = lax.broadcasted_iota(jnp.int32, (128,128), 1)
                    blk = jnp.where(i >= j, blk, 0.0)
                out[pl.ds(128*c, n), pl.ds(128*t, w)] = blk[:n, :w]
    copy.wait()

def chol(packed, con):
    return pl.pallas_call(
        chol_kernel, name="chol",
        out_shape=(jax.ShapeDtypeStruct((I2, I2), F32), jax.ShapeDtypeStruct(con.shape, F32)),
        in_specs=[pl.BlockSpec(memory_space=pltpu.VMEM), pl.BlockSpec(memory_space=pl.ANY)],
        out_specs=(pl.BlockSpec(memory_space=pltpu.VMEM), pl.BlockSpec(memory_space=pl.ANY)),
        scratch_shapes=[pltpu.VMEM((4, 512, 128), F32), pltpu.SemaphoreType.DMA],
        compiler_params=pltpu.CompilerParams(vmem_limit_bytes=32*2**20),
    )(packed, con)


def local(slab, factor_one):
    contracted, packed = exchange(slab.transpose(1, 0, 2), factor_one.T)
    lower_factor, contracted = chol(packed.reshape(PACKED, LANES), contracted)
    return (contracted, lower_factor)


def solution(mesh):
    return jax.shard_map(
        local,
        mesh=mesh,
        in_specs=(P(None, "gx", "yz"), P()),
        out_specs=(P("gx", None, "yz"), P()),
        check_vma=False,
    )
```

```python
import jax
import jax.numpy as jnp
from jax import lax
from jax.experimental import pallas as pl
from jax.experimental.pallas import tpu as pltpu
from jax.sharding import PartitionSpec as P

I1, I2, R1 = 500, 480, 96
GX, YZ = 32, 16
KPAD = 512
JB = I2 // GX
RB = R1 // GX
LANES = 128
COLS = (0, 480, 832, 1056)
PACKED = 1152
HALF = 640
PIECE = HALF // YZ
TILES = PIECE // 8
NZ = GX // 2
BF = jnp.bfloat16
F32 = jnp.float32


def split(x):
    hi = x.astype(BF)
    return hi, (x - hi.astype(F32)).astype(BF)


def dot(a, b):
    return lax.dot_general(a, b, (((1,), (0,)), ((), ())), preferred_element_type=F32)


def dot_nt(a, b):
    return lax.dot_general(a, b, (((1,), (1,)), ((), ())), preferred_element_type=F32)


def far_first(me, k, n):
    step = (k + 1) // 2
    off = n // 2 + jnp.where(k % 2 == 1, -step, step)
    return lax.rem(me + off, n)


def exchange_kernel(
    slab, ft, con, full,
    slab_a, slab_b, ft_in, ft_v, send_a, send_b, got_a, got_b, gram, got_h, half, got_y, mine, got_z, total,
    load_sem, sa_sem, ra_sem, sb_sem, rb_sem, core_sem, sy_sem, ry_sem, sz_sem, rz_sem, sg_sem, rg_sem, sf_sem, rf_sem,
    sh_sem, rh_sem,
):
    gx = lax.axis_index("gx")
    yz = lax.axis_index("yz")
    z = gx // 2
    core = lax.rem(gx, 2)
    partner = gx + 1 - 2 * core

    load_f = pltpu.make_async_copy(ft, ft_in, load_sem.at[2])
    load_a = pltpu.make_async_copy(slab.at[pl.ds(0, 8)], slab_a.at[:, pl.ds(0, I1), :], load_sem.at[0])
    load_b = pltpu.make_async_copy(slab.at[pl.ds(8, JB - 8)], slab_b.at[:, pl.ds(0, I1), :], load_sem.at[1])
    load_f.start()
    load_a.start()
    load_b.start()

    barrier = pltpu.get_barrier_semaphore()

    @pl.loop(0, GX - 1)
    def _(k):
        pl.semaphore_signal(barrier, inc=1, device_id={"gx": far_first(gx, k, GX)}, device_id_type=pl.DeviceIdType.MESH)

    @pl.loop(1, YZ)
    def _(d):
        pl.semaphore_signal(barrier, inc=1, device_id={"yz": lax.rem(yz + d, YZ)}, device_id_type=pl.DeviceIdType.MESH)

    slab_a[:, pl.ds(I1, KPAD - I1), :] = jnp.zeros((8, KPAD - I1, LANES), F32)
    slab_b[:, pl.ds(I1, KPAD - I1), :] = jnp.zeros((JB - 8, KPAD - I1, LANES), F32)
    ft_v[:, pl.ds(KPAD - LANES, LANES)] = jnp.zeros((R1, LANES), F32)
    gram[pl.ds(COLS[3], 2 * HALF - COLS[3]), :] = jnp.zeros((2 * HALF - COLS[3], LANES), F32)
    load_f.wait()
    ft_v[:, pl.ds(0, I1)] = ft_in[...]
    f_hi, f_lo = split(ft_v[...])
    f_both = jnp.concatenate([f_hi, f_lo], axis=0)

    def contract(src, dst, count):
        for j in range(0, count, 2):
            js = [j] if j + 1 == count else [j, j + 1]
            s = [src[q] for q in js]
            s = s[0] if len(s) == 1 else jnp.concatenate(s, axis=1)
            s_hi, s_lo = split(s)
            two = dot(f_both, s_hi)
            res = two[:R1] + (two[R1:] + dot(f_hi, s_lo))
            for n, q in enumerate(js):
                dst[:, q, :] = res[:, n * LANES:(n + 1) * LANES]

    def copy_a(to):
        return pltpu.make_async_remote_copy(
            src_ref=send_a.at[pl.ds(to * RB, RB)], dst_ref=got_a.at[gx],
            send_sem=sa_sem.at[to], recv_sem=ra_sem.at[gx],
            device_id={"gx": to}, device_id_type=pl.DeviceIdType.MESH)

    def copy_b(to):
        return pltpu.make_async_remote_copy(
            src_ref=send_b.at[pl.ds(to * RB, RB)], dst_ref=got_b.at[gx],
            send_sem=sb_sem.at[to], recv_sem=rb_sem.at[gx],
            device_id={"gx": to}, device_id_type=pl.DeviceIdType.MESH)

    def from_a(at):
        return pltpu.make_async_remote_copy(
            src_ref=send_a.at[pl.ds(at * RB, RB)], dst_ref=got_a.at[at],
            send_sem=sa_sem.at[at], recv_sem=ra_sem.at[at],
            device_id={"gx": at}, device_id_type=pl.DeviceIdType.MESH)

    def from_b(at):
        return pltpu.make_async_remote_copy(
            src_ref=send_b.at[pl.ds(at * RB, RB)], dst_ref=got_b.at[at],
            send_sem=sb_sem.at[at], recv_sem=rb_sem.at[at],
            device_id={"gx": at}, device_id_type=pl.DeviceIdType.MESH)

    load_a.wait()
    contract(slab_a, send_a, 8)
    pl.semaphore_wait(barrier, GX - 1 + YZ - 1)

    @pl.loop(0, GX - 1)
    def _(k):
        copy_a(far_first(gx, k, GX)).start()

    load_b.wait()
    contract(slab_b, send_b, JB - 8)

    @pl.loop(0, GX - 1)
    def _(k):
        copy_b(far_first(gx, k, GX)).start()

    for r in range(RB):
        con[r, pl.ds(JB * gx, 8), :] = send_a[gx * RB + r]
        con[r, pl.ds(JB * gx + 8, JB - 8), :] = send_b[gx * RB + r]

    @pl.loop(0, GX - 1)
    def _(k):
        at = far_first(gx, k, GX)
        from_a(at).wait_recv()
        from_b(at).wait_recv()
        for r in range(RB):
            con[r, pl.ds(JB * at, 8), :] = got_a[at, r]
            con[r, pl.ds(JB * at + 8, JB - 8), :] = got_b[at, r]

    hi, lo = split(jnp.concatenate([con[r] for r in range(RB)], axis=1))
    for c, at in enumerate(COLS):
        rows = I2 - LANES * c
        a = slice(LANES * c, I2)
        b = slice(LANES * c, min(LANES * (c + 1), I2))
        gram[pl.ds(at, rows), pl.ds(0, min(rows, LANES))] = dot_nt(hi[a], hi[b]) + (dot_nt(hi[a], lo[b]) + dot_nt(lo[a], hi[b]))

    swap = pltpu.make_async_remote_copy(
        src_ref=gram.at[pl.ds(pl.multiple_of((1 - core) * HALF, 8), HALF)], dst_ref=got_h,
        send_sem=core_sem.at[0], recv_sem=core_sem.at[1],
        device_id={"gx": partner}, device_id_type=pl.DeviceIdType.MESH)
    swap.start()
    swap.wait_recv()
    half[...] = gram[pl.ds(pl.multiple_of(core * HALF, 8), HALF), :] + got_h[...]

    def copy_y(to):
        return pltpu.make_async_remote_copy(
            src_ref=half.at[pl.ds(pl.multiple_of(to * PIECE, 8), PIECE)], dst_ref=got_y.at[yz],
            send_sem=sy_sem.at[to], recv_sem=ry_sem.at[yz],
            device_id={"yz": to}, device_id_type=pl.DeviceIdType.MESH)

    def from_y(at):
        return pltpu.make_async_remote_copy(
            src_ref=half.at[pl.ds(pl.multiple_of(at * PIECE, 8), PIECE)], dst_ref=got_y.at[at],
            send_sem=sy_sem.at[at], recv_sem=ry_sem.at[at],
            device_id={"yz": at}, device_id_type=pl.DeviceIdType.MESH)

    @pl.loop(1, YZ)
    def _(d):
        copy_y(lax.rem(yz + d, YZ)).start()

    got_y[yz] = half[pl.ds(pl.multiple_of(yz * PIECE, 8), PIECE), :]

    @pl.loop(1, YZ)
    def _(d):
        from_y(lax.rem(yz + d, YZ)).wait_recv()

    mine[...] = jnp.sum(got_y[...], axis=0)

    def copy_z(t):
        return pltpu.make_async_remote_copy(
            src_ref=mine.at[pl.ds(pl.multiple_of(t * 8, 8), 8)], dst_ref=got_z.at[z],
            send_sem=sz_sem.at[t], recv_sem=rz_sem.at[z],
            device_id={"gx": 6 * t + core}, device_id_type=pl.DeviceIdType.MESH)

    def from_z(at):
        return pltpu.make_async_remote_copy(
            src_ref=mine.at[pl.ds(0, 8)], dst_ref=got_z.at[at],
            send_sem=sz_sem.at[0], recv_sem=rz_sem.at[at],
            device_id={"gx": 2 * at + core}, device_id_type=pl.DeviceIdType.MESH)

    owner = jnp.logical_and(lax.rem(z, 3) == 0, z < 3 * TILES)
    tile = z // 3

    @pl.loop(0, TILES)
    def _(t):
        @pl.when(z != 3 * t)
        def _():
            copy_z(t).start()

    def spread(to):
        return pltpu.make_async_remote_copy(
            src_ref=total.at[tile], dst_ref=total.at[tile],
            send_sem=sg_sem.at[to], recv_sem=rg_sem.at[tile],
            device_id={"gx": 2 * to + core}, device_id_type=pl.DeviceIdType.MESH)

    def from_owner(t):
        return pltpu.make_async_remote_copy(
            src_ref=total.at[t], dst_ref=total.at[t],
            send_sem=sg_sem.at[0], recv_sem=rg_sem.at[t],
            device_id={"gx": 6 * t + core}, device_id_type=pl.DeviceIdType.MESH)

    @pl.when(owner)
    def _():
        got_z[z] = mine[pl.ds(pl.multiple_of(tile * 8, 8), 8), :]

        @pl.loop(1, NZ)
        def _(d):
            from_z(lax.rem(z + d, NZ)).wait_recv()

        total[tile] = jnp.sum(got_z[...], axis=0) * (1.0 / (R1 * 2048))

        @pl.loop(0, NZ - 1)
        def _(k):
            spread(far_first(z, k, NZ)).start()

    @pl.loop(0, TILES)
    def _(t):
        @pl.when(z != 3 * t)
        def _():
            from_owner(t).wait_recv()

    def copy_f(to):
        return pltpu.make_async_remote_copy(
            src_ref=total, dst_ref=full.at[core, yz],
            send_sem=sf_sem.at[to], recv_sem=rf_sem.at[yz],
            device_id={"yz": to}, device_id_type=pl.DeviceIdType.MESH)

    def from_f(at):
        return pltpu.make_async_remote_copy(
            src_ref=total, dst_ref=full.at[core, at],
            send_sem=sf_sem.at[at], recv_sem=rf_sem.at[at],
            device_id={"yz": at}, device_id_type=pl.DeviceIdType.MESH)

    def hand(at):
        return pltpu.make_async_remote_copy(
            src_ref=full.at[core, at], dst_ref=full.at[core, at],
            send_sem=sh_sem.at[at], recv_sem=rh_sem.at[at],
            device_id={"gx": partner}, device_id_type=pl.DeviceIdType.MESH)

    def handed(at):
        return pltpu.make_async_remote_copy(
            src_ref=full.at[1 - core, at], dst_ref=full.at[1 - core, at],
            send_sem=sh_sem.at[at], recv_sem=rh_sem.at[at],
            device_id={"gx": partner}, device_id_type=pl.DeviceIdType.MESH)

    @pl.loop(1, YZ)
    def _(d):
        copy_f(lax.rem(yz + d, YZ)).start()

    full[core, yz] = total[...]
    hand(yz).start()

    @pl.loop(1, YZ)
    def _(d):
        at = lax.rem(yz + d, YZ)
        from_f(at).wait_recv()
        hand(at).start()

    swap.wait_send()

    @pl.loop(1, GX)
    def _(d):
        to = lax.rem(gx + d, GX)
        copy_a(to).wait_send()
        copy_b(to).wait_send()

    @pl.when(owner)
    def _():
        @pl.loop(1, NZ)
        def _(d):
            spread(lax.rem(z + d, NZ)).wait_send()

    @pl.loop(0, TILES)
    def _(t):
        @pl.when(z != 3 * t)
        def _():
            copy_z(t).wait_send()

    @pl.loop(1, YZ)
    def _(d):
        to = lax.rem(yz + d, YZ)
        copy_y(to).wait_send()
        copy_f(to).wait_send()

    @pl.loop(0, YZ)
    def _(at):
        handed(at).wait_recv()
        hand(at).wait_send()


def exchange(slab, ft):
    dma = pltpu.SemaphoreType.DMA
    return pl.pallas_call(
        exchange_kernel,
        name="exchange",
        out_shape=(
            jax.ShapeDtypeStruct((RB, I2, LANES), F32),
            jax.ShapeDtypeStruct((2, YZ, TILES, 8, LANES), F32),
        ),
        in_specs=[pl.BlockSpec(memory_space=pltpu.HBM)] * 2,
        out_specs=(pl.BlockSpec(memory_space=pltpu.VMEM),) * 2,
        scratch_shapes=[
            pltpu.VMEM((8, KPAD, LANES), F32),
            pltpu.VMEM((JB - 8, KPAD, LANES), F32),
            pltpu.VMEM((R1, I1), F32),
            pltpu.VMEM((R1, KPAD), F32),
            pltpu.VMEM((R1, 8, LANES), F32),
            pltpu.VMEM((R1, JB - 8, LANES), F32),
            pltpu.VMEM((GX, RB, 8, LANES), F32),
            pltpu.VMEM((GX, RB, JB - 8, LANES), F32),
            pltpu.VMEM((2 * HALF, LANES), F32),
            pltpu.VMEM((HALF, LANES), F32),
            pltpu.VMEM((HALF, LANES), F32),
            pltpu.VMEM((YZ, PIECE, LANES), F32),
            pltpu.VMEM((PIECE, LANES), F32),
            pltpu.VMEM((NZ, 8, LANES), F32),
            pltpu.VMEM((TILES, 8, LANES), F32),
            dma((3,)),
            dma((GX,)), dma((GX,)), dma((GX,)), dma((GX,)),
            dma((2,)),
            dma((YZ,)), dma((YZ,)),
            dma((TILES,)), dma((NZ,)),
            dma((NZ,)), dma((TILES,)),
            dma((YZ,)), dma((YZ,)),
            dma((YZ,)), dma((YZ,)),
        ],
        compiler_params=pltpu.CompilerParams(
            collective_id=0, has_side_effects=True, vmem_limit_bytes=52 * 2**20
        ),
    )(slab, ft)


def outer(a, b):
    ah, al = split(a)
    bh, bl = split(b)
    lhs = jnp.concatenate([ah, ah, al], axis=0)
    rhs = jnp.concatenate([bh, bl, bh], axis=0)
    return lax.dot_general(lhs, rhs, (((0,), (0,)), ((), ())), preferred_element_type=F32)

def factor_rows(diag, rest, lane):
    tiles = [diag] + rest
    rows = [[x[8*p:8*p+8] for p in range(4)] for x in tiles]
    sub = lax.broadcasted_iota(jnp.int32, (8, LANES), 0)
    done = [[] for _ in tiles]
    cols = [[jnp.broadcast_to(rows[0][q][:, lane+k:lane+k+1], (8, LANES)) for q in range(k // 8, 4)] for k in range(32)]
    fin = [[rows[t][p] for p in range(4)] for t in range(len(tiles))]
    for k in range(32):
        p, kr = divmod(k, 8)
        piv = jnp.broadcast_to(cols[k][0][kr:kr+1], (8, LANES))
        rs = lax.rsqrt(piv)
        inv = rs * rs
        c0 = jnp.where(sub > kr, cols[k][0], 0.0)
        cs = [c0] + cols[k][1:]
        for kk in range(k+1, 32):
            pp, kkr = divmod(kk, 8)
            w = jnp.broadcast_to(cols[k][pp-p][kkr:kkr+1], (8, LANES)) * inv
            cols[kk] = [cols[kk][q] - cs[q + pp - p] * w for q in range(4 - pp)]
        for t in range(len(tiles)):
            r = jnp.broadcast_to(rows[t][p][kr:kr+1], (8, LANES))
            fin[t][p] = jnp.where(sub == kr, r * rs, fin[t][p])
            ri = r * inv
            for q in range(p, 4):
                rows[t][q] = rows[t][q] - cs[q-p] * ri
    done = fin
    return [jnp.concatenate(d, axis=0) for d in done]

def chol_kernel(packed, con, out, con_out, sem):
    copy = pltpu.make_async_copy(con, con_out, sem)
    copy.start()
    tri = lax.broadcasted_iota(jnp.int32, (128, 128), 0) >= lax.broadcasted_iota(jnp.int32, (128, 128), 1)
    A = {}
    for c in range(4):
        for t in range(c, 4):
            n = min(128, I2 - 128*t)
            blk = packed[pl.ds(COLS[c] + 128*(t-c), n), :]
            if n < 128:
                blk = jnp.concatenate([blk, jnp.zeros((128-n, 128), F32)], axis=0)
            A[c, t] = blk.T
    for c in range(4):
        subs = 3 if c == 3 else 4
        cur = [A[c, t] for t in range(c, 4)]
        fin = [[] for _ in cur]
        for sb in range(subs):
            u = factor_rows(cur[0][:32], [x[:32] for x in cur[1:]], 32*sb)
            for f, x in zip(fin, u):
                f.append(x)
            if sb + 1 < subs:
                lhs = u[0][:, 32*(sb+1):32*subs]
                upd = outer(lhs, jnp.concatenate(u, axis=1))
                cur = [x[32:32*subs-32*sb] - upd[:, 128*t:128*(t+1)] for t, x in enumerate(cur)]
        U = [jnp.concatenate(f, axis=0) for f in fin]
        n = 32*subs
        for t in range(c, 4):
            w = min(128, I2 - 128*t)
            blk = U[t-c]
            if n < 128:
                blk = jnp.concatenate([blk, jnp.zeros((128-n, 128), F32)], axis=0)
            blk = blk.T
            if t == c:
                blk = jnp.where(tri, blk, 0.0)
            out[pl.ds(128*t, w), pl.ds(128*c, n)] = blk[:w, :n]
        for t in range(c+1, 4):
            w = min(128, I2 - 128*t)
            out[pl.ds(128*c, n), pl.ds(128*t, w)] = jnp.zeros((n, w), F32)
        for d in range(c+1, 4):
            upd = outer(U[d-c], jnp.concatenate(U[d-c:], axis=1) if d < 3 else U[d-c])
            for t in range(d, 4):
                A[d, t] = A[d, t] - upd[:, 128*(t-d):128*(t-d+1)]
    copy.wait()


def chol(packed, con):
    return pl.pallas_call(
        chol_kernel, name="chol",
        out_shape=(jax.ShapeDtypeStruct((I2, I2), F32), jax.ShapeDtypeStruct(con.shape, F32)),
        in_specs=[pl.BlockSpec(memory_space=pltpu.VMEM), pl.BlockSpec(memory_space=pl.ANY)],
        out_specs=(pl.BlockSpec(memory_space=pltpu.VMEM), pl.BlockSpec(memory_space=pl.ANY)),
        scratch_shapes=[pltpu.SemaphoreType.DMA],
        compiler_params=pltpu.CompilerParams(vmem_limit_bytes=32*2**20),
    )(packed, con)


def local(slab, factor_one):
    contracted, packed = exchange(slab.transpose(1, 0, 2), factor_one.T)
    lower_factor, contracted = chol(packed.reshape(2 * HALF, LANES), contracted)
    return (contracted, lower_factor)


def solution(mesh):
    return jax.shard_map(
        local,
        mesh=mesh,
        in_specs=(P(None, "gx", "yz"), P()),
        out_specs=(P("gx", None, "yz"), P()),
        check_vma=False,
    )
```

```python
import jax
import jax.numpy as jnp
from jax import lax
from jax.experimental import pallas as pl
from jax.experimental.pallas import tpu as pltpu
from jax.sharding import PartitionSpec as P

I1, I2, R1 = 500, 480, 96
GX, YZ = 32, 16
KPAD = 512
JB = I2 // GX
RB = R1 // GX
LANES = 128
SUB = 32
WIDE = 16
COLS = (0, 480, 832, 1056)
PACKED = 1152
HALF = 640
PIECE = HALF // YZ
TILES = PIECE // 8
NZ = GX // 2
BF = jnp.bfloat16
F32 = jnp.float32


def split(x):
    hi = x.astype(BF)
    return hi, (x - hi.astype(F32)).astype(BF)


def dot(a, b):
    return lax.dot_general(a, b, (((1,), (0,)), ((), ())), preferred_element_type=F32)


def dot_nt(a, b):
    return lax.dot_general(a, b, (((1,), (1,)), ((), ())), preferred_element_type=F32)


def far_first(me, k, n):
    step = (k + 1) // 2
    off = n // 2 + jnp.where(k % 2 == 1, -step, step)
    return lax.rem(me + off, n)


def exchange_kernel(
    slab, ft, con, full,
    slab_a, slab_b, ft_in, ft_v, send, got, gram, got_h, half, got_y, mine, got_z, total,
    load_sem, sa_sem, ra_sem, core_sem, sy_sem, ry_sem, sz_sem, rz_sem, sg_sem, rg_sem, sf_sem, rf_sem,
    sh_sem, rh_sem,
):
    gx = lax.axis_index("gx")
    yz = lax.axis_index("yz")
    z = gx // 2
    core = lax.rem(gx, 2)
    partner = gx + 1 - 2 * core

    load_f = pltpu.make_async_copy(ft, ft_in, load_sem.at[2])
    load_a = pltpu.make_async_copy(slab.at[pl.ds(0, 8)], slab_a.at[:, pl.ds(0, I1), :], load_sem.at[0])
    load_b = pltpu.make_async_copy(slab.at[pl.ds(8, JB - 8)], slab_b.at[:, pl.ds(0, I1), :], load_sem.at[1])
    load_f.start()
    load_a.start()
    load_b.start()

    barrier = pltpu.get_barrier_semaphore()

    @pl.loop(0, GX - 1)
    def _(k):
        pl.semaphore_signal(barrier, inc=1, device_id={"gx": far_first(gx, k, GX)}, device_id_type=pl.DeviceIdType.MESH)

    @pl.loop(1, YZ)
    def _(d):
        pl.semaphore_signal(barrier, inc=1, device_id={"yz": lax.rem(yz + d, YZ)}, device_id_type=pl.DeviceIdType.MESH)

    slab_a[:, pl.ds(I1, KPAD - I1), :] = jnp.zeros((8, KPAD - I1, LANES), F32)
    slab_b[:, pl.ds(I1, KPAD - I1), :] = jnp.zeros((JB - 8, KPAD - I1, LANES), F32)
    ft_v[:, pl.ds(KPAD - LANES, LANES)] = jnp.zeros((R1, LANES), F32)
    gram[pl.ds(COLS[3], 2 * HALF - COLS[3]), :] = jnp.zeros((2 * HALF - COLS[3], LANES), F32)
    load_f.wait()
    ft_v[:, pl.ds(0, I1)] = ft_in[...]
    f_hi, f_lo = split(ft_v[...])
    f_both = jnp.concatenate([f_hi, f_lo], axis=0)

    def contract(src, first, count):
        for j in range(0, count, 2):
            js = [j] if j + 1 == count else [j, j + 1]
            s = [src[q] for q in js]
            s = s[0] if len(s) == 1 else jnp.concatenate(s, axis=1)
            s_hi, s_lo = split(s)
            two = dot(f_both, s_hi)
            res = two[:R1] + (two[R1:] + dot(f_hi, s_lo))
            for n, q in enumerate(js):
                send[:, first + q, :] = res[:, n * LANES:(n + 1) * LANES]

    def copy_a(to):
        return pltpu.make_async_remote_copy(
            src_ref=send.at[pl.ds(to * RB, RB)], dst_ref=got.at[gx],
            send_sem=sa_sem.at[to], recv_sem=ra_sem.at[gx],
            device_id={"gx": to}, device_id_type=pl.DeviceIdType.MESH)

    def from_a(at):
        return pltpu.make_async_remote_copy(
            src_ref=send.at[pl.ds(at * RB, RB)], dst_ref=got.at[at],
            send_sem=sa_sem.at[at], recv_sem=ra_sem.at[at],
            device_id={"gx": at}, device_id_type=pl.DeviceIdType.MESH)

    load_a.wait()
    contract(slab_a, 0, 8)
    load_b.wait()
    contract(slab_b, 8, JB - 8)
    pl.semaphore_wait(barrier, GX - 1 + YZ - 1)

    @pl.loop(0, GX - 1)
    def _(k):
        copy_a(far_first(gx, k, GX)).start()

    for r in range(RB):
        con[r, pl.ds(JB * gx, JB), :] = send[gx * RB + r]

    @pl.loop(0, GX - 1)
    def _(k):
        at = far_first(gx, k, GX)
        from_a(at).wait_recv()
        for r in range(RB):
            con[r, pl.ds(JB * at, JB), :] = got[at, r]

    hi, lo = split(jnp.concatenate([con[r] for r in range(RB)], axis=1))
    for c, at in enumerate(COLS):
        rows = I2 - LANES * c
        a = slice(LANES * c, I2)
        b = slice(LANES * c, min(LANES * (c + 1), I2))
        gram[pl.ds(at, rows), pl.ds(0, min(rows, LANES))] = dot_nt(hi[a], hi[b]) + (dot_nt(hi[a], lo[b]) + dot_nt(lo[a], hi[b]))

    swap = pltpu.make_async_remote_copy(
        src_ref=gram.at[pl.ds(pl.multiple_of((1 - core) * HALF, 8), HALF)], dst_ref=got_h,
        send_sem=core_sem.at[0], recv_sem=core_sem.at[1],
        device_id={"gx": partner}, device_id_type=pl.DeviceIdType.MESH)
    swap.start()
    swap.wait_recv()
    half[...] = gram[pl.ds(pl.multiple_of(core * HALF, 8), HALF), :] + got_h[...]

    def copy_y(to):
        return pltpu.make_async_remote_copy(
            src_ref=half.at[pl.ds(pl.multiple_of(to * PIECE, 8), PIECE)], dst_ref=got_y.at[yz],
            send_sem=sy_sem.at[to], recv_sem=ry_sem.at[yz],
            device_id={"yz": to}, device_id_type=pl.DeviceIdType.MESH)

    def from_y(at):
        return pltpu.make_async_remote_copy(
            src_ref=half.at[pl.ds(pl.multiple_of(at * PIECE, 8), PIECE)], dst_ref=got_y.at[at],
            send_sem=sy_sem.at[at], recv_sem=ry_sem.at[at],
            device_id={"yz": at}, device_id_type=pl.DeviceIdType.MESH)

    @pl.loop(1, YZ)
    def _(d):
        copy_y(lax.rem(yz + d, YZ)).start()

    got_y[yz] = half[pl.ds(pl.multiple_of(yz * PIECE, 8), PIECE), :]

    @pl.loop(1, YZ)
    def _(d):
        from_y(lax.rem(yz + d, YZ)).wait_recv()

    mine[...] = jnp.sum(got_y[...], axis=0)

    def copy_z(t):
        return pltpu.make_async_remote_copy(
            src_ref=mine.at[pl.ds(pl.multiple_of(t * 8, 8), 8)], dst_ref=got_z.at[z],
            send_sem=sz_sem.at[t], recv_sem=rz_sem.at[z],
            device_id={"gx": 6 * t + core}, device_id_type=pl.DeviceIdType.MESH)

    def from_z(at):
        return pltpu.make_async_remote_copy(
            src_ref=mine.at[pl.ds(0, 8)], dst_ref=got_z.at[at],
            send_sem=sz_sem.at[0], recv_sem=rz_sem.at[at],
            device_id={"gx": 2 * at + core}, device_id_type=pl.DeviceIdType.MESH)

    owner = jnp.logical_and(lax.rem(z, 3) == 0, z < 3 * TILES)
    tile = z // 3

    @pl.loop(0, TILES)
    def _(t):
        @pl.when(z != 3 * t)
        def _():
            copy_z(t).start()

    swap.wait_send()

    @pl.loop(1, GX)
    def _(d):
        copy_a(lax.rem(gx + d, GX)).wait_send()

    @pl.loop(1, YZ)
    def _(d):
        copy_y(lax.rem(yz + d, YZ)).wait_send()

    def spread(to):
        return pltpu.make_async_remote_copy(
            src_ref=total.at[tile], dst_ref=total.at[tile],
            send_sem=sg_sem.at[to], recv_sem=rg_sem.at[tile],
            device_id={"gx": 2 * to + core}, device_id_type=pl.DeviceIdType.MESH)

    def from_owner(t):
        return pltpu.make_async_remote_copy(
            src_ref=total.at[t], dst_ref=total.at[t],
            send_sem=sg_sem.at[0], recv_sem=rg_sem.at[t],
            device_id={"gx": 6 * t + core}, device_id_type=pl.DeviceIdType.MESH)

    @pl.when(owner)
    def _():
        got_z[z] = mine[pl.ds(pl.multiple_of(tile * 8, 8), 8), :]

        @pl.loop(1, NZ)
        def _(d):
            from_z(lax.rem(z + d, NZ)).wait_recv()

        total[tile] = jnp.sum(got_z[...], axis=0) * (1.0 / (R1 * 2048))

        @pl.loop(0, NZ - 1)
        def _(k):
            spread(far_first(z, k, NZ)).start()

    @pl.loop(0, TILES)
    def _(t):
        @pl.when(z != 3 * t)
        def _():
            from_owner(t).wait_recv()

    def copy_f(to):
        return pltpu.make_async_remote_copy(
            src_ref=total, dst_ref=full.at[core, yz],
            send_sem=sf_sem.at[to], recv_sem=rf_sem.at[yz],
            device_id={"yz": to}, device_id_type=pl.DeviceIdType.MESH)

    def from_f(at):
        return pltpu.make_async_remote_copy(
            src_ref=total, dst_ref=full.at[core, at],
            send_sem=sf_sem.at[at], recv_sem=rf_sem.at[at],
            device_id={"yz": at}, device_id_type=pl.DeviceIdType.MESH)

    def hand(at):
        return pltpu.make_async_remote_copy(
            src_ref=full.at[core, at], dst_ref=full.at[core, at],
            send_sem=sh_sem.at[at], recv_sem=rh_sem.at[at],
            device_id={"gx": partner}, device_id_type=pl.DeviceIdType.MESH)

    def handed(at):
        return pltpu.make_async_remote_copy(
            src_ref=full.at[1 - core, at], dst_ref=full.at[1 - core, at],
            send_sem=sh_sem.at[at], recv_sem=rh_sem.at[at],
            device_id={"gx": partner}, device_id_type=pl.DeviceIdType.MESH)

    @pl.loop(1, YZ)
    def _(d):
        copy_f(lax.rem(yz + d, YZ)).start()

    full[core, yz] = total[...]
    hand(yz).start()

    @pl.when(owner)
    def _():
        @pl.loop(1, NZ)
        def _(d):
            spread(lax.rem(z + d, NZ)).wait_send()

    @pl.loop(0, TILES)
    def _(t):
        @pl.when(z != 3 * t)
        def _():
            copy_z(t).wait_send()

    @pl.loop(1, YZ)
    def _(d):
        at = lax.rem(yz + d, YZ)
        from_f(at).wait_recv()
        hand(at).start()

    @pl.loop(1, YZ)
    def _(d):
        copy_f(lax.rem(yz + d, YZ)).wait_send()

    @pl.loop(0, YZ)
    def _(at):
        handed(at).wait_recv()
        hand(at).wait_send()


def exchange(slab, ft):
    dma = pltpu.SemaphoreType.DMA
    return pl.pallas_call(
        exchange_kernel,
        name="exchange",
        out_shape=(
            jax.ShapeDtypeStruct((RB, I2, LANES), F32),
            jax.ShapeDtypeStruct((2, YZ, TILES, 8, LANES), F32),
        ),
        in_specs=[pl.BlockSpec(memory_space=pltpu.HBM)] * 2,
        out_specs=(pl.BlockSpec(memory_space=pltpu.VMEM),) * 2,
        scratch_shapes=[
            pltpu.VMEM((8, KPAD, LANES), F32),
            pltpu.VMEM((JB - 8, KPAD, LANES), F32),
            pltpu.VMEM((R1, I1), F32),
            pltpu.VMEM((R1, KPAD), F32),
            pltpu.VMEM((R1, JB, LANES), F32),
            pltpu.VMEM((GX, RB, JB, LANES), F32),
            pltpu.VMEM((2 * HALF, LANES), F32),
            pltpu.VMEM((HALF, LANES), F32),
            pltpu.VMEM((HALF, LANES), F32),
            pltpu.VMEM((YZ, PIECE, LANES), F32),
            pltpu.VMEM((PIECE, LANES), F32),
            pltpu.VMEM((NZ, 8, LANES), F32),
            pltpu.VMEM((TILES, 8, LANES), F32),
            dma((3,)),
            dma((GX,)), dma((GX,)),
            dma((2,)),
            dma((YZ,)), dma((YZ,)),
            dma((TILES,)), dma((NZ,)),
            dma((NZ,)), dma((TILES,)),
            dma((YZ,)), dma((YZ,)),
            dma((YZ,)), dma((YZ,)),
        ],
        compiler_params=pltpu.CompilerParams(
            collective_id=0, has_side_effects=True, vmem_limit_bytes=52 * 2**20
        ),
    )(slab, ft)


def outer(a, b):
    ah, al = split(a)
    bh, bl = split(b)
    lhs = jnp.concatenate([ah, ah, al], axis=0)
    rhs = jnp.concatenate([bh, bl, bh], axis=0)
    return lax.dot_general(lhs, rhs, (((0,), (0,)), ((), ())), preferred_element_type=F32)

def factor_rows(diag, rest, lane):
    tiles = [diag] + rest
    n = diag.shape[0]
    nt = n // 8
    rows = [[x[8*p:8*p+8] for p in range(nt)] for x in tiles]
    sub = lax.broadcasted_iota(jnp.int32, (8, LANES), 0)
    fin = [[None] * nt for _ in tiles]
    for start in range(0, n, WIDE):
        top = start // 8
        cols = {k: {q: jnp.broadcast_to(rows[0][q][:, lane+k:lane+k+1], (8, LANES)) for q in range(k // 8, nt)}
                for k in range(start, start + WIDE)}
        for k in range(start, start + WIDE):
            p, kr = divmod(k, 8)
            piv = jnp.broadcast_to(cols[k][p][kr:kr+1], (8, LANES))
            rs = lax.rsqrt(piv)
            inv = rs * rs
            cs = dict(cols[k])
            cs[p] = jnp.where(sub > kr, cs[p], 0.0)
            for kk in range(k+1, start + WIDE):
                pp, kkr = divmod(kk, 8)
                w = jnp.broadcast_to(cols[k][pp][kkr:kkr+1], (8, LANES)) * inv
                cols[kk] = {q: cols[kk][q] - cs[q] * w for q in cols[kk]}
            for t in range(len(tiles)):
                r = jnp.broadcast_to(rows[t][p][kr:kr+1], (8, LANES))
                u = r * rs
                fin[t][p] = u if kr == 0 else jnp.where(sub == kr, u, fin[t][p])
                ri = r * inv
                for q in range(p, nt):
                    rows[t][q] = rows[t][q] - cs[q] * ri
    return [jnp.concatenate(d, axis=0) for d in fin]


def chol_kernel(packed, con, out, con_out, low, sem):
    copy = pltpu.make_async_copy(con, con_out, sem.at[4])
    copy.start()
    tri = lax.broadcasted_iota(jnp.int32, (128, 128), 0) >= lax.broadcasted_iota(jnp.int32, (128, 128), 1)
    A = {}
    writes = []
    for c in range(4):
        for t in range(c, 4):
            n = min(128, I2 - 128*t)
            blk = packed[pl.ds(COLS[c] + 128*(t-c), n), :]
            if n < 128:
                blk = jnp.concatenate([blk, jnp.zeros((128-n, 128), F32)], axis=0)
            A[c, t] = blk.T
    for c in range(4):
        n = min(128, I2 - 128*c)
        cur = [A[c, t][:n] for t in range(c, 4)]
        fin = [[] for _ in cur]
        at = 0
        while at < n:
            m = min(SUB, n - at)
            u = factor_rows(cur[0][:m], [x[:m] for x in cur[1:]], at)
            for f, x in zip(fin, u):
                f.append(x)
            at += m
            if at < n:
                upd = outer(u[0][:, at:n], jnp.concatenate(u, axis=1))
                cur = [x[m:] - upd[:, 128*t:128*(t+1)] for t, x in enumerate(cur)]
        U = [jnp.concatenate(f, axis=0) for f in fin]
        for t in range(c, 4):
            w = min(128, I2 - 128*t)
            blk = U[t-c]
            if n < 128:
                blk = jnp.concatenate([blk, jnp.zeros((128-n, 128), F32)], axis=0)
            blk = blk.T
            if t == c:
                blk = jnp.where(tri, blk, 0.0)
            low[pl.ds(128*t, w), pl.ds(128*c, n)] = blk[:w, :n]
        for t in range(c+1, 4):
            w = min(128, I2 - 128*t)
            low[pl.ds(128*c, n), pl.ds(128*t, w)] = jnp.zeros((n, w), F32)
        rows = pl.ds(128*c, n)
        writes.append(pltpu.make_async_copy(low.at[rows], out.at[rows], sem.at[c]))
        writes[-1].start()
        for d in range(c+1, 4):
            upd = outer(U[d-c], jnp.concatenate(U[d-c:], axis=1) if d < 3 else U[d-c])
            for t in range(d, 4):
                A[d, t] = A[d, t] - upd[:, 128*(t-d):128*(t-d+1)]
    for w in writes:
        w.wait()
    copy.wait()


def chol(packed, con):
    return pl.pallas_call(
        chol_kernel, name="chol",
        out_shape=(jax.ShapeDtypeStruct((I2, I2), F32), jax.ShapeDtypeStruct(con.shape, F32)),
        in_specs=[pl.BlockSpec(memory_space=pltpu.VMEM), pl.BlockSpec(memory_space=pl.ANY)],
        out_specs=(pl.BlockSpec(memory_space=pl.ANY),) * 2,
        scratch_shapes=[pltpu.VMEM((I2, I2), F32), pltpu.SemaphoreType.DMA((5,))],
        compiler_params=pltpu.CompilerParams(vmem_limit_bytes=32*2**20),
    )(packed, con)


def local(slab, factor_one):
    in_hbm = lambda x: pltpu.with_memory_space_constraint(x, pltpu.HBM)
    contracted, packed = exchange(in_hbm(slab.transpose(1, 0, 2)), in_hbm(factor_one.T))
    lower_factor, contracted = chol(packed.reshape(2 * HALF, LANES), contracted)
    return (contracted, lower_factor)


def solution(mesh):
    return jax.shard_map(
        local,
        mesh=mesh,
        in_specs=(P(None, "gx", "yz"), P()),
        out_specs=(P("gx", None, "yz"), P()),
        check_vma=False,
    )
```

```python
import jax
import jax.numpy as jnp
from jax import lax
from jax.experimental import pallas as pl
from jax.experimental.pallas import tpu as pltpu
from jax.sharding import PartitionSpec as P

I1, I2, R1 = 500, 480, 96
GX, YZ = 32, 16
KPAD = 512
JB = I2 // GX
RB = R1 // GX
LANES = 128
SUB = 32
WIDE = 16
COLS = (0, 480, 832, 1056)
PACKED = 1152
HALF = 640
PIECE = HALF // YZ
TILES = PIECE // 8
NZ = GX // 2
BF = jnp.bfloat16
F32 = jnp.float32


def split(x):
    hi = x.astype(BF)
    return hi, (x - hi.astype(F32)).astype(BF)


def dot(a, b):
    return lax.dot_general(a, b, (((1,), (0,)), ((), ())), preferred_element_type=F32)


def dot_nt(a, b):
    return lax.dot_general(a, b, (((1,), (1,)), ((), ())), preferred_element_type=F32)


def far_first(me, k, n):
    step = (k + 1) // 2
    off = n // 2 + jnp.where(k % 2 == 1, -step, step)
    return lax.rem(me + off, n)


def exchange_kernel(
    slab, ft, con, full,
    slab_a, slab_b, ft_in, ft_v, send, got, gram, got_h, half, got_y, mine, got_z, total,
    load_sem, sa_sem, ra_sem, core_sem, sy_sem, ry_sem, sz_sem, rz_sem, sg_sem, rg_sem, sf_sem, rf_sem,
    sh_sem, rh_sem,
):
    gx = lax.axis_index("gx")
    yz = lax.axis_index("yz")
    z = gx // 2
    core = lax.rem(gx, 2)
    partner = gx + 1 - 2 * core

    load_f = pltpu.make_async_copy(ft, ft_in, load_sem.at[2])
    load_a = pltpu.make_async_copy(slab.at[pl.ds(0, 8)], slab_a.at[:, pl.ds(0, I1), :], load_sem.at[0])
    load_b = pltpu.make_async_copy(slab.at[pl.ds(8, JB - 8)], slab_b.at[:, pl.ds(0, I1), :], load_sem.at[1])
    load_f.start()
    load_a.start()
    load_b.start()

    barrier = pltpu.get_barrier_semaphore()

    @pl.loop(0, GX - 1)
    def _(k):
        pl.semaphore_signal(barrier, inc=1, device_id={"gx": far_first(gx, k, GX)}, device_id_type=pl.DeviceIdType.MESH)

    @pl.loop(1, YZ)
    def _(d):
        pl.semaphore_signal(barrier, inc=1, device_id={"yz": lax.rem(yz + d, YZ)}, device_id_type=pl.DeviceIdType.MESH)

    slab_a[:, pl.ds(I1, KPAD - I1), :] = jnp.zeros((8, KPAD - I1, LANES), F32)
    slab_b[:, pl.ds(I1, KPAD - I1), :] = jnp.zeros((JB - 8, KPAD - I1, LANES), F32)
    ft_v[:, pl.ds(KPAD - LANES, LANES)] = jnp.zeros((R1, LANES), F32)
    gram[pl.ds(COLS[3], 2 * HALF - COLS[3]), :] = jnp.zeros((2 * HALF - COLS[3], LANES), F32)
    load_f.wait()
    ft_v[:, pl.ds(0, I1)] = ft_in[...]
    f_hi, f_lo = split(ft_v[...])
    f_both = jnp.concatenate([f_hi, f_lo], axis=0)

    def contract(src, first, count):
        for j in range(0, count, 2):
            js = [j] if j + 1 == count else [j, j + 1]
            s = [src[q] for q in js]
            s = s[0] if len(s) == 1 else jnp.concatenate(s, axis=1)
            s_hi, s_lo = split(s)
            two = dot(f_both, s_hi)
            res = two[:R1] + (two[R1:] + dot(f_hi, s_lo))
            for n, q in enumerate(js):
                send[:, first + q, :] = res[:, n * LANES:(n + 1) * LANES]

    def copy_a(to):
        return pltpu.make_async_remote_copy(
            src_ref=send.at[pl.ds(to * RB, RB)], dst_ref=got.at[gx],
            send_sem=sa_sem.at[to], recv_sem=ra_sem.at[gx],
            device_id={"gx": to}, device_id_type=pl.DeviceIdType.MESH)

    def from_a(at):
        return pltpu.make_async_remote_copy(
            src_ref=send.at[pl.ds(at * RB, RB)], dst_ref=got.at[at],
            send_sem=sa_sem.at[at], recv_sem=ra_sem.at[at],
            device_id={"gx": at}, device_id_type=pl.DeviceIdType.MESH)

    load_a.wait()
    contract(slab_a, 0, 8)
    load_b.wait()
    contract(slab_b, 8, JB - 8)
    pl.semaphore_wait(barrier, GX - 1 + YZ - 1)

    @pl.loop(0, GX - 1)
    def _(k):
        copy_a(far_first(gx, k, GX)).start()

    for r in range(RB):
        con[r, pl.ds(JB * gx, JB), :] = send[gx * RB + r]

    @pl.loop(0, GX - 1)
    def _(k):
        at = far_first(gx, k, GX)
        from_a(at).wait_recv()
        for r in range(RB):
            con[r, pl.ds(JB * at, JB), :] = got[at, r]

    hi, lo = split(jnp.concatenate([con[r] for r in range(RB)], axis=1))
    for c, at in enumerate(COLS):
        rows = I2 - LANES * c
        a = slice(LANES * c, I2)
        b = slice(LANES * c, min(LANES * (c + 1), I2))
        gram[pl.ds(at, rows), pl.ds(0, min(rows, LANES))] = dot_nt(hi[a], hi[b]) + (dot_nt(hi[a], lo[b]) + dot_nt(lo[a], hi[b]))

    swap = pltpu.make_async_remote_copy(
        src_ref=gram.at[pl.ds(pl.multiple_of((1 - core) * HALF, 8), HALF)], dst_ref=got_h,
        send_sem=core_sem.at[0], recv_sem=core_sem.at[1],
        device_id={"gx": partner}, device_id_type=pl.DeviceIdType.MESH)
    swap.start()
    swap.wait_recv()
    half[...] = gram[pl.ds(pl.multiple_of(core * HALF, 8), HALF), :] + got_h[...]

    def copy_y(to):
        return pltpu.make_async_remote_copy(
            src_ref=half.at[pl.ds(pl.multiple_of(to * PIECE, 8), PIECE)], dst_ref=got_y.at[yz],
            send_sem=sy_sem.at[to], recv_sem=ry_sem.at[yz],
            device_id={"yz": to}, device_id_type=pl.DeviceIdType.MESH)

    def from_y(at):
        return pltpu.make_async_remote_copy(
            src_ref=half.at[pl.ds(pl.multiple_of(at * PIECE, 8), PIECE)], dst_ref=got_y.at[at],
            send_sem=sy_sem.at[at], recv_sem=ry_sem.at[at],
            device_id={"yz": at}, device_id_type=pl.DeviceIdType.MESH)

    @pl.loop(1, YZ)
    def _(d):
        copy_y(lax.rem(yz + d, YZ)).start()

    got_y[yz] = half[pl.ds(pl.multiple_of(yz * PIECE, 8), PIECE), :]

    @pl.loop(1, YZ)
    def _(d):
        from_y(lax.rem(yz + d, YZ)).wait_recv()

    mine[...] = jnp.sum(got_y[...], axis=0)

    def owner_of(k):
        return lax.rem(3 * (k // 2) + (NZ // 2) * lax.rem(k, 2), NZ)

    def copy_z(k):
        return pltpu.make_async_remote_copy(
            src_ref=mine.at[pl.ds(pl.multiple_of((k // 2) * 8, 8), 8)], dst_ref=got_z.at[z],
            send_sem=sz_sem.at[k], recv_sem=rz_sem.at[z],
            device_id={"gx": 2 * owner_of(k) + core}, device_id_type=pl.DeviceIdType.MESH)

    def from_z(at):
        return pltpu.make_async_remote_copy(
            src_ref=mine.at[pl.ds(0, 8)], dst_ref=got_z.at[at],
            send_sem=sz_sem.at[0], recv_sem=rz_sem.at[at],
            device_id={"gx": 2 * at + core}, device_id_type=pl.DeviceIdType.MESH)

    first = jnp.logical_and(lax.rem(z, 3) == 0, z < 3 * TILES)
    seat = jnp.where(first, z, lax.rem(z + NZ // 2, NZ))
    owner = jnp.logical_and(lax.rem(seat, 3) == 0, seat < 3 * TILES)
    tile = seat // 3

    @pl.loop(0, 2 * TILES)
    def _(k):
        @pl.when(z != owner_of(k))
        def _():
            copy_z(k).start()

    swap.wait_send()

    @pl.loop(1, GX)
    def _(d):
        copy_a(lax.rem(gx + d, GX)).wait_send()

    @pl.loop(1, YZ)
    def _(d):
        copy_y(lax.rem(yz + d, YZ)).wait_send()

    def served(d):
        return lax.rem(z + NZ - 5 + d + jnp.where(d > 4, 1, 0), NZ)

    def nearest(t):
        near = lax.rem(z + NZ - 3 * t + NZ // 4, NZ) < NZ // 2
        return jnp.where(near, 3 * t, lax.rem(3 * t + NZ // 2, NZ))

    def spread(to):
        return pltpu.make_async_remote_copy(
            src_ref=total.at[tile], dst_ref=total.at[tile],
            send_sem=sg_sem.at[to], recv_sem=rg_sem.at[tile],
            device_id={"gx": 2 * to + core}, device_id_type=pl.DeviceIdType.MESH)

    def from_owner(t):
        return pltpu.make_async_remote_copy(
            src_ref=total.at[t], dst_ref=total.at[t],
            send_sem=sg_sem.at[0], recv_sem=rg_sem.at[t],
            device_id={"gx": 2 * nearest(t) + core}, device_id_type=pl.DeviceIdType.MESH)

    @pl.when(owner)
    def _():
        got_z[z] = mine[pl.ds(pl.multiple_of(tile * 8, 8), 8), :]

        @pl.loop(1, NZ)
        def _(d):
            from_z(lax.rem(z + d, NZ)).wait_recv()

        total[tile] = jnp.sum(got_z[...], axis=0) * (1.0 / (R1 * 2048))

        @pl.loop(1, NZ // 2)
        def _(d):
            spread(served(d)).start()

    @pl.loop(0, TILES)
    def _(t):
        @pl.when(z != nearest(t))
        def _():
            from_owner(t).wait_recv()

    def copy_f(to):
        return pltpu.make_async_remote_copy(
            src_ref=total, dst_ref=full.at[core, yz],
            send_sem=sf_sem.at[to], recv_sem=rf_sem.at[yz],
            device_id={"yz": to}, device_id_type=pl.DeviceIdType.MESH)

    def from_f(at):
        return pltpu.make_async_remote_copy(
            src_ref=total, dst_ref=full.at[core, at],
            send_sem=sf_sem.at[at], recv_sem=rf_sem.at[at],
            device_id={"yz": at}, device_id_type=pl.DeviceIdType.MESH)

    def hand(at):
        return pltpu.make_async_remote_copy(
            src_ref=full.at[core, at], dst_ref=full.at[core, at],
            send_sem=sh_sem.at[at], recv_sem=rh_sem.at[at],
            device_id={"gx": partner}, device_id_type=pl.DeviceIdType.MESH)

    def handed(at):
        return pltpu.make_async_remote_copy(
            src_ref=full.at[1 - core, at], dst_ref=full.at[1 - core, at],
            send_sem=sh_sem.at[at], recv_sem=rh_sem.at[at],
            device_id={"gx": partner}, device_id_type=pl.DeviceIdType.MESH)

    @pl.loop(1, YZ)
    def _(d):
        copy_f(lax.rem(yz + d, YZ)).start()

    full[core, yz] = total[...]
    hand(yz).start()

    @pl.when(owner)
    def _():
        @pl.loop(1, NZ // 2)
        def _(d):
            spread(served(d)).wait_send()

    @pl.loop(0, 2 * TILES)
    def _(k):
        @pl.when(z != owner_of(k))
        def _():
            copy_z(k).wait_send()

    @pl.loop(1, YZ)
    def _(d):
        at = lax.rem(yz + d, YZ)
        from_f(at).wait_recv()
        hand(at).start()

    @pl.loop(1, YZ)
    def _(d):
        copy_f(lax.rem(yz + d, YZ)).wait_send()

    @pl.loop(0, YZ)
    def _(at):
        handed(at).wait_recv()
        hand(at).wait_send()


def exchange(slab, ft):
    dma = pltpu.SemaphoreType.DMA
    return pl.pallas_call(
        exchange_kernel,
        name="exchange",
        out_shape=(
            jax.ShapeDtypeStruct((RB, I2, LANES), F32),
            jax.ShapeDtypeStruct((2, YZ, TILES, 8, LANES), F32),
        ),
        in_specs=[pl.BlockSpec(memory_space=pltpu.HBM)] * 2,
        out_specs=(pl.BlockSpec(memory_space=pltpu.VMEM),) * 2,
        scratch_shapes=[
            pltpu.VMEM((8, KPAD, LANES), F32),
            pltpu.VMEM((JB - 8, KPAD, LANES), F32),
            pltpu.VMEM((R1, I1), F32),
            pltpu.VMEM((R1, KPAD), F32),
            pltpu.VMEM((R1, JB, LANES), F32),
            pltpu.VMEM((GX, RB, JB, LANES), F32),
            pltpu.VMEM((2 * HALF, LANES), F32),
            pltpu.VMEM((HALF, LANES), F32),
            pltpu.VMEM((HALF, LANES), F32),
            pltpu.VMEM((YZ, PIECE, LANES), F32),
            pltpu.VMEM((PIECE, LANES), F32),
            pltpu.VMEM((NZ, 8, LANES), F32),
            pltpu.VMEM((TILES, 8, LANES), F32),
            dma((3,)),
            dma((GX,)), dma((GX,)),
            dma((2,)),
            dma((YZ,)), dma((YZ,)),
            dma((2 * TILES,)), dma((NZ,)),
            dma((NZ,)), dma((TILES,)),
            dma((YZ,)), dma((YZ,)),
            dma((YZ,)), dma((YZ,)),
        ],
        compiler_params=pltpu.CompilerParams(
            collective_id=0, has_side_effects=True, vmem_limit_bytes=52 * 2**20
        ),
    )(slab, ft)


def outer(a, b):
    ah, al = split(a)
    bh, bl = split(b)
    lhs = jnp.concatenate([ah, ah, al], axis=0)
    rhs = jnp.concatenate([bh, bl, bh], axis=0)
    return lax.dot_general(lhs, rhs, (((0,), (0,)), ((), ())), preferred_element_type=F32)

def factor_rows(diag, rest, lane):
    tiles = [diag] + rest
    n = diag.shape[0]
    nt = n // 8
    rows = [[x[8*p:8*p+8] for p in range(nt)] for x in tiles]
    sub = lax.broadcasted_iota(jnp.int32, (8, LANES), 0)
    fin = [[None] * nt for _ in tiles]
    for start in range(0, n, WIDE):
        top = start // 8
        cols = {k: {q: jnp.broadcast_to(rows[0][q][:, lane+k:lane+k+1], (8, LANES)) for q in range(k // 8, nt)}
                for k in range(start, start + WIDE)}
        for k in range(start, start + WIDE):
            p, kr = divmod(k, 8)
            piv = jnp.broadcast_to(cols[k][p][kr:kr+1], (8, LANES))
            rs = lax.rsqrt(piv)
            inv = rs * rs
            cs = dict(cols[k])
            cs[p] = jnp.where(sub > kr, cs[p], 0.0)
            for kk in range(k+1, start + WIDE):
                pp, kkr = divmod(kk, 8)
                w = jnp.broadcast_to(cols[k][pp][kkr:kkr+1], (8, LANES)) * inv
                cols[kk] = {q: cols[kk][q] - cs[q] * w for q in cols[kk]}
            for t in range(len(tiles)):
                r = jnp.broadcast_to(rows[t][p][kr:kr+1], (8, LANES))
                u = r * rs
                fin[t][p] = u if kr == 0 else jnp.where(sub == kr, u, fin[t][p])
                ri = r * inv
                for q in range(p, nt):
                    rows[t][q] = rows[t][q] - cs[q] * ri
    return [jnp.concatenate(d, axis=0) for d in fin]


def chol_kernel(packed, con, out, con_out, low, sem):
    copy = pltpu.make_async_copy(con, con_out, sem.at[4])
    copy.start()
    tri = lax.broadcasted_iota(jnp.int32, (128, 128), 0) >= lax.broadcasted_iota(jnp.int32, (128, 128), 1)
    A = {}
    writes = []
    for c in range(4):
        for t in range(c, 4):
            n = min(128, I2 - 128*t)
            blk = packed[pl.ds(COLS[c] + 128*(t-c), n), :]
            if n < 128:
                blk = jnp.concatenate([blk, jnp.zeros((128-n, 128), F32)], axis=0)
            A[c, t] = blk if t == c else blk.T
    for c in range(4):
        n = min(128, I2 - 128*c)
        cur = [A[c, t][:n] for t in range(c, 4)]
        fin = [[] for _ in cur]
        at = 0
        while at < n:
            m = min(SUB, n - at)
            u = factor_rows(cur[0][:m], [x[:m] for x in cur[1:]], at)
            for f, x in zip(fin, u):
                f.append(x)
            at += m
            if at < n:
                upd = outer(u[0][:, at:n], jnp.concatenate(u, axis=1))
                cur = [x[m:] - upd[:, 128*t:128*(t+1)] for t, x in enumerate(cur)]
        U = [jnp.concatenate(f, axis=0) for f in fin]
        for t in range(c, 4):
            w = min(128, I2 - 128*t)
            blk = U[t-c]
            if n < 128:
                blk = jnp.concatenate([blk, jnp.zeros((128-n, 128), F32)], axis=0)
            blk = blk.T
            if t == c:
                blk = jnp.where(tri, blk, 0.0)
            low[pl.ds(128*t, w), pl.ds(128*c, n)] = blk[:w, :n]
        for t in range(c+1, 4):
            w = min(128, I2 - 128*t)
            low[pl.ds(128*c, n), pl.ds(128*t, w)] = jnp.zeros((n, w), F32)
        rows = pl.ds(128*c, n)
        writes.append(pltpu.make_async_copy(low.at[rows], out.at[rows], sem.at[c]))
        writes[-1].start()
        for d in range(c+1, 4):
            upd = outer(U[d-c], jnp.concatenate(U[d-c:], axis=1) if d < 3 else U[d-c])
            for t in range(d, 4):
                A[d, t] = A[d, t] - upd[:, 128*(t-d):128*(t-d+1)]
    for w in writes:
        w.wait()
    copy.wait()


def chol(packed, con):
    return pl.pallas_call(
        chol_kernel, name="chol",
        out_shape=(jax.ShapeDtypeStruct((I2, I2), F32), jax.ShapeDtypeStruct(con.shape, F32)),
        in_specs=[pl.BlockSpec(memory_space=pltpu.VMEM), pl.BlockSpec(memory_space=pl.ANY)],
        out_specs=(pl.BlockSpec(memory_space=pl.ANY),) * 2,
        scratch_shapes=[pltpu.VMEM((I2, I2), F32), pltpu.SemaphoreType.DMA((5,))],
        compiler_params=pltpu.CompilerParams(vmem_limit_bytes=32*2**20),
    )(packed, con)


def local(slab, factor_one):
    in_hbm = lambda x: pltpu.with_memory_space_constraint(x, pltpu.HBM)
    contracted, packed = exchange(in_hbm(slab.transpose(1, 0, 2)), in_hbm(factor_one.T))
    lower_factor, contracted = chol(packed.reshape(2 * HALF, LANES), contracted)
    return (contracted, lower_factor)


def solution(mesh):
    return jax.shard_map(
        local,
        mesh=mesh,
        in_specs=(P(None, "gx", "yz"), P()),
        out_specs=(P("gx", None, "yz"), P()),
        check_vma=False,
    )
```

```python
import jax
import jax.numpy as jnp
from jax import lax
from jax.experimental import pallas as pl
from jax.experimental.pallas import tpu as pltpu
from jax.sharding import PartitionSpec as P

I1, I2, R1 = 500, 480, 96
GX, YZ = 32, 16
KPAD = 512
JB = I2 // GX
RB = R1 // GX
LANES = 128
SUB = 32
WIDE = 16
COLS = (0, 480, 832, 1056)
PACKED = 1152
HALF = 640
PIECE = HALF // YZ
TILES = PIECE // 8
NZ = GX // 2
BF = jnp.bfloat16
F32 = jnp.float32


def split(x):
    hi = x.astype(BF)
    return hi, (x - hi.astype(F32)).astype(BF)


def dot(a, b):
    return lax.dot_general(a, b, (((1,), (0,)), ((), ())), preferred_element_type=F32)


def dot_nt(a, b):
    return lax.dot_general(a, b, (((1,), (1,)), ((), ())), preferred_element_type=F32)


def far_first(me, k, n):
    step = (k + 1) // 2
    off = n // 2 + jnp.where(k % 2 == 1, -step, step)
    return lax.rem(me + off, n)


def exchange_kernel(
    slab, ft, con, full,
    slab_a, slab_b, ft_in, ft_v, send, got, gram, got_h, half, got_y, mine, got_z, total,
    load_sem, sa_sem, ra_sem, core_sem, sy_sem, ry_sem, sz_sem, rz_sem, sg_sem, rg_sem, sf_sem, rf_sem,
    sh_sem, rh_sem,
):
    gx = lax.axis_index("gx")
    yz = lax.axis_index("yz")
    z = gx // 2
    core = lax.rem(gx, 2)
    partner = gx + 1 - 2 * core

    load_f = pltpu.make_async_copy(ft, ft_in, load_sem.at[2])
    load_a = pltpu.make_async_copy(slab.at[pl.ds(0, 8)], slab_a.at[:, pl.ds(0, I1), :], load_sem.at[0])
    load_b = pltpu.make_async_copy(slab.at[pl.ds(8, JB - 8)], slab_b.at[:, pl.ds(0, I1), :], load_sem.at[1])
    load_f.start()
    load_a.start()
    load_b.start()

    barrier = pltpu.get_barrier_semaphore()

    @pl.loop(0, GX - 1)
    def _(k):
        pl.semaphore_signal(barrier, inc=1, device_id={"gx": far_first(gx, k, GX)}, device_id_type=pl.DeviceIdType.MESH)

    @pl.loop(1, YZ)
    def _(d):
        pl.semaphore_signal(barrier, inc=1, device_id={"yz": lax.rem(yz + d, YZ)}, device_id_type=pl.DeviceIdType.MESH)

    slab_a[:, pl.ds(I1, KPAD - I1), :] = jnp.zeros((8, KPAD - I1, LANES), F32)
    slab_b[:, pl.ds(I1, KPAD - I1), :] = jnp.zeros((JB - 8, KPAD - I1, LANES), F32)
    ft_v[:, pl.ds(KPAD - LANES, LANES)] = jnp.zeros((R1, LANES), F32)
    gram[pl.ds(COLS[3], 2 * HALF - COLS[3]), :] = jnp.zeros((2 * HALF - COLS[3], LANES), F32)
    load_f.wait()
    ft_v[:, pl.ds(0, I1)] = ft_in[...]
    f_hi, f_lo = split(ft_v[...])
    f_both = jnp.concatenate([f_hi, f_lo], axis=0)

    def contract(src, first, count):
        for j in range(0, count, 2):
            js = [j] if j + 1 == count else [j, j + 1]
            s = [src[q] for q in js]
            s = s[0] if len(s) == 1 else jnp.concatenate(s, axis=1)
            s_hi, s_lo = split(s)
            two = dot(f_both, s_hi)
            res = two[:R1] + (two[R1:] + dot(f_hi, s_lo))
            for n, q in enumerate(js):
                send[:, first + q, :] = res[:, n * LANES:(n + 1) * LANES]

    def copy_a(to):
        return pltpu.make_async_remote_copy(
            src_ref=send.at[pl.ds(to * RB, RB)], dst_ref=got.at[gx],
            send_sem=sa_sem.at[to], recv_sem=ra_sem.at[gx],
            device_id={"gx": to}, device_id_type=pl.DeviceIdType.MESH)

    def from_a(at):
        return pltpu.make_async_remote_copy(
            src_ref=send.at[pl.ds(at * RB, RB)], dst_ref=got.at[at],
            send_sem=sa_sem.at[at], recv_sem=ra_sem.at[at],
            device_id={"gx": at}, device_id_type=pl.DeviceIdType.MESH)

    load_a.wait()
    contract(slab_a, 0, 8)
    load_b.wait()
    contract(slab_b, 8, JB - 8)
    pl.semaphore_wait(barrier, GX - 1 + YZ - 1)

    @pl.loop(0, GX - 1)
    def _(k):
        copy_a(far_first(gx, k, GX)).start()

    for r in range(RB):
        con[r, pl.ds(JB * gx, JB), :] = send[gx * RB + r]

    @pl.loop(0, GX - 1)
    def _(k):
        at = far_first(gx, k, GX)
        from_a(at).wait_recv()
        for r in range(RB):
            con[r, pl.ds(JB * at, JB), :] = got[at, r]

    hi, lo = split(jnp.concatenate([con[r] for r in range(RB)], axis=1))
    for c, at in enumerate(COLS):
        rows = I2 - LANES * c
        a = slice(LANES * c, I2)
        b = slice(LANES * c, min(LANES * (c + 1), I2))
        gram[pl.ds(at, rows), pl.ds(0, min(rows, LANES))] = dot_nt(hi[a], hi[b]) + (dot_nt(hi[a], lo[b]) + dot_nt(lo[a], hi[b]))

    swap = pltpu.make_async_remote_copy(
        src_ref=gram.at[pl.ds(pl.multiple_of((1 - core) * HALF, 8), HALF)], dst_ref=got_h,
        send_sem=core_sem.at[0], recv_sem=core_sem.at[1],
        device_id={"gx": partner}, device_id_type=pl.DeviceIdType.MESH)
    swap.start()
    swap.wait_recv()
    half[...] = gram[pl.ds(pl.multiple_of(core * HALF, 8), HALF), :] + got_h[...]

    def copy_y(to):
        return pltpu.make_async_remote_copy(
            src_ref=half.at[pl.ds(pl.multiple_of(to * PIECE, 8), PIECE)], dst_ref=got_y.at[yz],
            send_sem=sy_sem.at[to], recv_sem=ry_sem.at[yz],
            device_id={"yz": to}, device_id_type=pl.DeviceIdType.MESH)

    def from_y(at):
        return pltpu.make_async_remote_copy(
            src_ref=half.at[pl.ds(pl.multiple_of(at * PIECE, 8), PIECE)], dst_ref=got_y.at[at],
            send_sem=sy_sem.at[at], recv_sem=ry_sem.at[at],
            device_id={"yz": at}, device_id_type=pl.DeviceIdType.MESH)

    @pl.loop(1, YZ)
    def _(d):
        copy_y(lax.rem(yz + d, YZ)).start()

    got_y[yz] = half[pl.ds(pl.multiple_of(yz * PIECE, 8), PIECE), :]

    @pl.loop(1, YZ)
    def _(d):
        from_y(lax.rem(yz + d, YZ)).wait_recv()

    mine[...] = jnp.sum(got_y[...], axis=0)

    def owner_of(k):
        return k

    def copy_z(k):
        return pltpu.make_async_remote_copy(
            src_ref=mine.at[pl.ds(pl.multiple_of(lax.rem(k, TILES) * 8, 8), 8)], dst_ref=got_z.at[z],
            send_sem=sz_sem.at[k], recv_sem=rz_sem.at[z],
            device_id={"gx": 2 * owner_of(k) + core}, device_id_type=pl.DeviceIdType.MESH)

    def from_z(at):
        return pltpu.make_async_remote_copy(
            src_ref=mine.at[pl.ds(0, 8)], dst_ref=got_z.at[at],
            send_sem=sz_sem.at[0], recv_sem=rz_sem.at[at],
            device_id={"gx": 2 * at + core}, device_id_type=pl.DeviceIdType.MESH)

    owner = z < 3 * TILES
    tile = lax.rem(z, TILES)

    @pl.loop(0, 3 * TILES)
    def _(k):
        @pl.when(z != owner_of(k))
        def _():
            copy_z(k).start()

    swap.wait_send()

    @pl.loop(1, GX)
    def _(d):
        copy_a(lax.rem(gx + d, GX)).wait_send()

    @pl.loop(1, YZ)
    def _(d):
        copy_y(lax.rem(yz + d, YZ)).wait_send()

    def served(d):
        return lax.rem(z + NZ - 2 + d + jnp.where(d > 1, 1, 0), NZ)

    last = jnp.where(z >= 2 * TILES, TILES, TILES - 1)

    def nearest(t):
        off = lax.rem(z + NZ - t + 2, NZ)
        return t + jnp.where(off < 5, 0, jnp.where(off < 10, 5, 10))

    def spread(to):
        return pltpu.make_async_remote_copy(
            src_ref=total.at[tile], dst_ref=total.at[tile],
            send_sem=sg_sem.at[to], recv_sem=rg_sem.at[tile],
            device_id={"gx": 2 * to + core}, device_id_type=pl.DeviceIdType.MESH)

    def from_owner(t):
        return pltpu.make_async_remote_copy(
            src_ref=total.at[t], dst_ref=total.at[t],
            send_sem=sg_sem.at[0], recv_sem=rg_sem.at[t],
            device_id={"gx": 2 * nearest(t) + core}, device_id_type=pl.DeviceIdType.MESH)

    @pl.when(owner)
    def _():
        got_z[z] = mine[pl.ds(pl.multiple_of(tile * 8, 8), 8), :]

        @pl.loop(1, NZ)
        def _(d):
            from_z(lax.rem(z + d, NZ)).wait_recv()

        total[tile] = jnp.sum(got_z[...], axis=0) * (1.0 / (R1 * 2048))

        @pl.loop(0, last)
        def _(d):
            spread(served(d)).start()

    @pl.loop(0, TILES)
    def _(t):
        @pl.when(z != nearest(t))
        def _():
            from_owner(t).wait_recv()

    def copy_f(to):
        return pltpu.make_async_remote_copy(
            src_ref=total, dst_ref=full.at[core, yz],
            send_sem=sf_sem.at[to], recv_sem=rf_sem.at[yz],
            device_id={"yz": to}, device_id_type=pl.DeviceIdType.MESH)

    def from_f(at):
        return pltpu.make_async_remote_copy(
            src_ref=total, dst_ref=full.at[core, at],
            send_sem=sf_sem.at[at], recv_sem=rf_sem.at[at],
            device_id={"yz": at}, device_id_type=pl.DeviceIdType.MESH)

    def hand(at):
        return pltpu.make_async_remote_copy(
            src_ref=full.at[core, at], dst_ref=full.at[core, at],
            send_sem=sh_sem.at[at], recv_sem=rh_sem.at[at],
            device_id={"gx": partner}, device_id_type=pl.DeviceIdType.MESH)

    def handed(at):
        return pltpu.make_async_remote_copy(
            src_ref=full.at[1 - core, at], dst_ref=full.at[1 - core, at],
            send_sem=sh_sem.at[at], recv_sem=rh_sem.at[at],
            device_id={"gx": partner}, device_id_type=pl.DeviceIdType.MESH)

    @pl.loop(1, YZ)
    def _(d):
        copy_f(lax.rem(yz + d, YZ)).start()

    full[core, yz] = total[...]
    hand(yz).start()

    @pl.when(owner)
    def _():
        @pl.loop(0, last)
        def _(d):
            spread(served(d)).wait_send()

    @pl.loop(0, 3 * TILES)
    def _(k):
        @pl.when(z != owner_of(k))
        def _():
            copy_z(k).wait_send()

    @pl.loop(1, YZ)
    def _(d):
        at = lax.rem(yz + d, YZ)
        from_f(at).wait_recv()
        hand(at).start()

    @pl.loop(1, YZ)
    def _(d):
        copy_f(lax.rem(yz + d, YZ)).wait_send()

    @pl.loop(0, YZ)
    def _(at):
        handed(at).wait_recv()
        hand(at).wait_send()


def exchange(slab, ft):
    dma = pltpu.SemaphoreType.DMA
    return pl.pallas_call(
        exchange_kernel,
        name="exchange",
        out_shape=(
            jax.ShapeDtypeStruct((RB, I2, LANES), F32),
            jax.ShapeDtypeStruct((2, YZ, TILES, 8, LANES), F32),
        ),
        in_specs=[pl.BlockSpec(memory_space=pltpu.HBM)] * 2,
        out_specs=(pl.BlockSpec(memory_space=pltpu.VMEM),) * 2,
        scratch_shapes=[
            pltpu.VMEM((8, KPAD, LANES), F32),
            pltpu.VMEM((JB - 8, KPAD, LANES), F32),
            pltpu.VMEM((R1, I1), F32),
            pltpu.VMEM((R1, KPAD), F32),
            pltpu.VMEM((R1, JB, LANES), F32),
            pltpu.VMEM((GX, RB, JB, LANES), F32),
            pltpu.VMEM((2 * HALF, LANES), F32),
            pltpu.VMEM((HALF, LANES), F32),
            pltpu.VMEM((HALF, LANES), F32),
            pltpu.VMEM((YZ, PIECE, LANES), F32),
            pltpu.VMEM((PIECE, LANES), F32),
            pltpu.VMEM((NZ, 8, LANES), F32),
            pltpu.VMEM((TILES, 8, LANES), F32),
            dma((3,)),
            dma((GX,)), dma((GX,)),
            dma((2,)),
            dma((YZ,)), dma((YZ,)),
            dma((3 * TILES,)), dma((NZ,)),
            dma((NZ,)), dma((TILES,)),
            dma((YZ,)), dma((YZ,)),
            dma((YZ,)), dma((YZ,)),
        ],
        compiler_params=pltpu.CompilerParams(
            collective_id=0, has_side_effects=True, vmem_limit_bytes=52 * 2**20
        ),
    )(slab, ft)


def outer(a, b):
    ah, al = split(a)
    bh, bl = split(b)
    lhs = jnp.concatenate([ah, ah, al], axis=0)
    rhs = jnp.concatenate([bh, bl, bh], axis=0)
    return lax.dot_general(lhs, rhs, (((0,), (0,)), ((), ())), preferred_element_type=F32)

def factor_rows(diag, rest, lane):
    tiles = [diag] + rest
    n = diag.shape[0]
    nt = n // 8
    rows = [[x[8*p:8*p+8] for p in range(nt)] for x in tiles]
    sub = lax.broadcasted_iota(jnp.int32, (8, LANES), 0)
    fin = [[None] * nt for _ in tiles]
    for start in range(0, n, WIDE):
        top = start // 8
        cols = {k: {q: jnp.broadcast_to(rows[0][q][:, lane+k:lane+k+1], (8, LANES)) for q in range(k // 8, nt)}
                for k in range(start, start + WIDE)}
        for k in range(start, start + WIDE):
            p, kr = divmod(k, 8)
            piv = jnp.broadcast_to(cols[k][p][kr:kr+1], (8, LANES))
            rs = lax.rsqrt(piv)
            inv = 1.0 / piv
            cs = dict(cols[k])
            cs[p] = jnp.where(sub > kr, cs[p], 0.0)
            for kk in range(k+1, start + WIDE):
                pp, kkr = divmod(kk, 8)
                w = jnp.broadcast_to(cols[k][pp][kkr:kkr+1], (8, LANES)) * inv
                cols[kk] = {q: cols[kk][q] - cs[q] * w for q in cols[kk]}
            for t in range(len(tiles)):
                r = jnp.broadcast_to(rows[t][p][kr:kr+1], (8, LANES))
                u = r * rs
                fin[t][p] = u if kr == 0 else jnp.where(sub == kr, u, fin[t][p])
                ri = r * inv
                for q in range(p, nt):
                    rows[t][q] = rows[t][q] - cs[q] * ri
    return [jnp.concatenate(d, axis=0) for d in fin]


def chol_kernel(packed, con, out, con_out, low, sem):
    copy = pltpu.make_async_copy(con, con_out, sem.at[4])
    copy.start()
    tri = lax.broadcasted_iota(jnp.int32, (128, 128), 0) >= lax.broadcasted_iota(jnp.int32, (128, 128), 1)
    A = {}
    writes = []
    for c in range(4):
        for t in range(c, 4):
            n = min(128, I2 - 128*t)
            blk = packed[pl.ds(COLS[c] + 128*(t-c), n), :]
            if n < 128:
                blk = jnp.concatenate([blk, jnp.zeros((128-n, 128), F32)], axis=0)
            A[c, t] = blk if t == c else blk.T
    for c in range(4):
        n = min(128, I2 - 128*c)
        cur = [A[c, t][:n] for t in range(c, 4)]
        fin = [[] for _ in cur]
        at = 0
        while at < n:
            m = min(SUB, n - at)
            u = factor_rows(cur[0][:m], [x[:m] for x in cur[1:]], at)
            for f, x in zip(fin, u):
                f.append(x)
            at += m
            if at < n:
                upd = outer(u[0][:, at:n], jnp.concatenate(u, axis=1))
                cur = [x[m:] - upd[:, 128*t:128*(t+1)] for t, x in enumerate(cur)]
        U = [jnp.concatenate(f, axis=0) for f in fin]
        for t in range(c, 4):
            w = min(128, I2 - 128*t)
            blk = U[t-c]
            if n < 128:
                blk = jnp.concatenate([blk, jnp.zeros((128-n, 128), F32)], axis=0)
            blk = blk.T
            if t == c:
                blk = jnp.where(tri, blk, 0.0)
            low[pl.ds(128*t, w), pl.ds(128*c, n)] = blk[:w, :n]
        for t in range(c+1, 4):
            w = min(128, I2 - 128*t)
            low[pl.ds(128*c, n), pl.ds(128*t, w)] = jnp.zeros((n, w), F32)
        rows = pl.ds(128*c, n)
        writes.append(pltpu.make_async_copy(low.at[rows], out.at[rows], sem.at[c]))
        writes[-1].start()
        for d in range(c+1, 4):
            upd = outer(U[d-c], jnp.concatenate(U[d-c:], axis=1) if d < 3 else U[d-c])
            for t in range(d, 4):
                A[d, t] = A[d, t] - upd[:, 128*(t-d):128*(t-d+1)]
    for w in writes:
        w.wait()
    copy.wait()


def chol(packed, con):
    return pl.pallas_call(
        chol_kernel, name="chol",
        out_shape=(jax.ShapeDtypeStruct((I2, I2), F32), jax.ShapeDtypeStruct(con.shape, F32)),
        in_specs=[pl.BlockSpec(memory_space=pltpu.VMEM), pl.BlockSpec(memory_space=pl.ANY)],
        out_specs=(pl.BlockSpec(memory_space=pl.ANY),) * 2,
        scratch_shapes=[pltpu.VMEM((I2, I2), F32), pltpu.SemaphoreType.DMA((5,))],
        compiler_params=pltpu.CompilerParams(vmem_limit_bytes=32*2**20),
    )(packed, con)


def local(slab, factor_one):
    in_hbm = lambda x: pltpu.with_memory_space_constraint(x, pltpu.HBM)
    contracted, packed = exchange(in_hbm(slab.transpose(1, 0, 2)), in_hbm(factor_one.T))
    lower_factor, contracted = chol(packed.reshape(2 * HALF, LANES), contracted)
    return (contracted, lower_factor)


def solution(mesh):
    return jax.shard_map(
        local,
        mesh=mesh,
        in_specs=(P(None, "gx", "yz"), P()),
        out_specs=(P("gx", None, "yz"), P()),
        check_vma=False,
    )
```
